32 devices in a mesh: rep: 8 (over y, x, core), fsdp: 4 (over z).
Axes of the slice: x: 2, y: 2, z: 4, core: 2. Of those that a mesh axis runs over, the one named last changes fastest.
Arguments:
- base: float32 [128, 8192], P('fsdp'), as said below
- local: bfloat16 [8, 128, 8192], P('rep', 'fsdp'), as said below
- momentum: float32 [128, 8192], P('fsdp'), may hold values from -3 to 3
- tokens: bfloat16 [8192, 128], P(('rep', 'fsdp')), may hold values from -0.5 to 0.5
Outputs:
- new_base: float32 [128, 8192], P('fsdp')
- new_momentum: float32 [128, 8192], P('fsdp')
- projected: bfloat16 [8192, 8192], P(('rep', 'fsdp'))
The draws below stay inside these ranges and needn't reach their ends.
Inputs may be any that keep to these rules, and one draw needn't show every extreme that they name: `base`: entries of order one. `local`: each replica's copy of the rows lies near base, by block-wise differing amounts.
All inputs are finite; a program needn't handle non-finite values. Where the reference program divides by a largest or mean magnitude, that divisor is 1e-20 or more.
Results may differ from the reference program's by a relative error of at most 0.008.
Values may be sent and summed in bfloat16 or wider, within the bound.
No kernel may reach another device: no remote copies, remote signals or barrier semaphores. Data moves between devices by JAX's collectives and lax.ppermute only.
A program may use at most 64 MiB of HBM per device.

```python
import math
import jax
import jax.numpy as jnp
from jax import lax

D = 8192
BLOCK = 128
ROWS = 128
TOKENS = 8192
N_REP = 8


def shared_base(key):
    return jax.random.normal(key, (ROWS, D), jnp.float32)


def draw_base(key, part):
    return shared_base(key)


def draw_local(key, part):
    base = shared_base(key)
    key = jax.random.fold_in(key, 7)
    rough = jax.random.normal(jax.random.fold_in(key, 1), (N_REP, ROWS, D), jnp.float32)
    levels = jax.random.uniform(jax.random.fold_in(key, 3), (N_REP, ROWS, D // BLOCK, 1), jnp.float32, math.log(0.05), math.log(0.5))
    spread = jnp.broadcast_to(jnp.exp(levels), (N_REP, ROWS, D // BLOCK, BLOCK)).reshape(N_REP, ROWS, D)
    noise = rough * spread
    return (base[None] + noise).astype(jnp.bfloat16)


def level_of(stream_key, dims, shards, smallest, largest):
    def one(dim, shards_of):
        steps = jax.random.uniform(jax.random.fold_in(jax.random.fold_in(stream_key, 6), dim), (shards_of,), jnp.float32, smallest / len(shards), largest / len(shards))
        return jnp.repeat(jnp.exp(steps), dims[dim] // shards_of).reshape((-1,) + (1,) * (len(dims) - dim - 1))

    gain = one(*shards[0])
    for cut in shards[1:]:
        gain = gain * one(*cut)
    return gain


def centred(rng, shape, scale, reach, pieces=(), kind=jnp.bfloat16):
    array = scale * jax.random.normal(rng, shape, jnp.float32)
    if pieces:
        array = array * level_of(rng, shape, pieces, -0.22, 0.18)
    return jnp.clip(array, -reach, reach).astype(kind)


def setup_inputs(seed: int = 0) -> dict:
    seeds = jax.random.split(jax.random.key(seed), 5)
    return {
        "base": draw_base(jax.random.fold_in(seeds[4], 71), 0),
        "local": draw_local(jax.random.fold_in(seeds[4], 71), 0),
        "momentum": centred(seeds[2], (ROWS, D), 0.5, 3.0, ((0, 4),), jnp.float32),
        "tokens": centred(seeds[3], (TOKENS, ROWS), ROWS ** -0.5, 0.5, ((0, 32),)),
    }


outer_lr = 0.7
outer_mu = 0.9


def decode_one(base, replica):
    delta = base - replica.astype(jnp.float32)
    blocks = delta.reshape(delta.shape[0], delta.shape[1] // BLOCK, BLOCK)
    scales = jnp.max(jnp.abs(blocks), axis=2) + 1e-6
    codes = (blocks / scales[:, :, None]).astype(jnp.bfloat16)
    codes = lax.optimization_barrier(codes)
    return (codes.astype(jnp.float32) * scales[:, :, None]).reshape(delta.shape)


def reference(base, local, momentum, tokens):
    def accumulate(total, replica):
        return total + decode_one(base, replica), None

    total, unused = lax.scan(accumulate, jnp.zeros(base.shape, jnp.float32), local)
    average = total / N_REP
    new_momentum = outer_mu * momentum + average
    new_base = base - outer_lr * (average + outer_mu * new_momentum)
    fresh = new_base.astype(jnp.bfloat16)
    projected = jnp.dot(tokens, fresh, preferred_element_type=jnp.float32).astype(jnp.bfloat16)
    return new_base, new_momentum, projected
```

```python
import functools

import jax
import jax.numpy as jnp
from jax import lax
from jax.experimental import pallas as pl
from jax.experimental.pallas import tpu as pltpu
from jax.sharding import PartitionSpec as P

BLOCK = 128
MIB = 1 << 20

outer_lr = 0.7
outer_mu = 0.9


def params(mib=8):
    return pltpu.CompilerParams(vmem_limit_bytes=mib * MIB)


def decoded_block(base, replica):
    delta = base - replica.astype(jnp.float32)
    scale = jnp.max(jnp.abs(delta), axis=1, keepdims=True) + 1e-06
    code = (delta / scale).astype(jnp.bfloat16)
    return (code.astype(jnp.float32) * scale).astype(jnp.bfloat16)


def encode_kernel(at_ref, base_ref, local_ref, out_ref):
    for b in range(base_ref.shape[1] // BLOCK):
        cols = slice(b * BLOCK, (b + 1) * BLOCK)
        out_ref[0, :, cols] = decoded_block(base_ref[:, cols], local_ref[0, :, cols])


def encode(at, base, local, flip, chips, width):
    rows = base.shape[0]
    return pl.pallas_call(
        encode_kernel,
        out_shape=jax.ShapeDtypeStruct((chips, rows, width), jnp.bfloat16),
        grid_spec=pltpu.PrefetchScalarGridSpec(
            num_scalar_prefetch=1,
            grid=(chips,),
            in_specs=[
                pl.BlockSpec((rows, width), lambda j, at: (0, at[0] ^ flip ^ (2 * j))),
                pl.BlockSpec((1, rows, width), lambda j, at: (0, 0, at[0] ^ flip ^ (2 * j))),
            ],
            out_specs=pl.BlockSpec((1, rows, width), lambda j, at: (j, 0, 0)),
        ),
        compiler_params=params(),
    )(at, base, local)


def chip_sum_kernel(keep_ref, recv_ref, *out_refs):
    for j, out_ref in enumerate(out_refs):
        total = keep_ref[j].astype(jnp.float32) + recv_ref[j].astype(jnp.float32)
        out_ref[...] = total.astype(out_ref.dtype)


def chip_sum(keep, recv):
    chips, rows, width = keep.shape
    return pl.pallas_call(
        chip_sum_kernel,
        out_shape=[
            jax.ShapeDtypeStruct((rows, width), jnp.float32 if j == 0 else jnp.bfloat16)
            for j in range(chips)
        ],
        compiler_params=params(),
    )(keep, recv)


def stepped(average, base, momentum):
    moved = outer_mu * momentum + average
    return base - outer_lr * (average + outer_mu * moved), moved


def chunk_step_kernel(replicas, at_ref, base_ref, mom_ref, own_ref, *refs):
    parts, (avg_ref, fresh_ref) = refs[:-2], refs[-2:]
    total = own_ref[...]
    for part in parts:
        total = total + part[...].astype(jnp.float32)
    average = (total / replicas).astype(jnp.bfloat16)
    avg_ref[...] = average
    new_base, _ = stepped(average.astype(jnp.float32), base_ref[...], mom_ref[...])
    fresh_ref[...] = new_base.astype(jnp.bfloat16)


def chunk_step(at, base, momentum, own, parts, replicas):
    rows, width = own.shape
    whole = pl.BlockSpec((rows, width), lambda i, at: (0, 0))
    mine = pl.BlockSpec((rows, width), lambda i, at: (0, at[0]))
    return pl.pallas_call(
        functools.partial(chunk_step_kernel, replicas),
        out_shape=[jax.ShapeDtypeStruct((rows, width), jnp.bfloat16)] * 2,
        grid_spec=pltpu.PrefetchScalarGridSpec(
            num_scalar_prefetch=1,
            grid=(1,),
            in_specs=[mine, mine, whole] + [whole] * len(parts),
            out_specs=[whole, whole],
        ),
        compiler_params=params(),
    )(at, base, momentum, own, *parts)


def outer_kernel(replicas, at_ref, base_ref, mom_ref, *refs):
    parts, (new_base_ref, new_mom_ref, fresh_ref) = refs[:replicas], refs[replicas:]
    for k, part in enumerate(parts):

        @pl.when(pl.program_id(0) == k)
        def _():
            new_base, moved = stepped(part[...].astype(jnp.float32), base_ref[...], mom_ref[...])
            new_base_ref[...] = new_base
            new_mom_ref[...] = moved
            fresh_ref[0] = new_base.astype(jnp.bfloat16)


def outer(at, base, momentum, averages):
    rows, width = averages[0].shape
    replicas = len(averages)
    whole = pl.BlockSpec((rows, width), lambda k, at: (0, 0))
    chunk = pl.BlockSpec((rows, width), lambda k, at: (0, at[0] ^ k))
    return pl.pallas_call(
        functools.partial(outer_kernel, replicas),
        out_shape=[
            jax.ShapeDtypeStruct(base.shape, jnp.float32),
            jax.ShapeDtypeStruct(base.shape, jnp.float32),
            jax.ShapeDtypeStruct((replicas, rows, width), jnp.bfloat16),
        ],
        grid_spec=pltpu.PrefetchScalarGridSpec(
            num_scalar_prefetch=1,
            grid=(replicas,),
            in_specs=[chunk, chunk] + [whole] * replicas,
            out_specs=[chunk, chunk, pl.BlockSpec((1, rows, width), lambda k, at: (k, 0, 0))],
        ),
        compiler_params=params(),
    )(at, base, momentum, *averages)


def project_kernel(replicas, at_ref, tok_ref, own_ref, *refs):
    parts, (out_ref, rhs_ref) = refs[:replicas], refs[replicas:]
    rows = own_ref.shape[1]
    here = at_ref[1]

    def place(s):
        return pl.ds(pl.multiple_of((here ^ s) * rows, rows), rows)

    rhs_ref[place(0), :] = own_ref[0]
    for k, part in enumerate(parts):

        @pl.when(pl.program_id(0) == k)
        def _():
            for s in range(part.shape[0] // rows):
                rhs_ref[place(s + 1), :] = part[s * rows : (s + 1) * rows, :]

    out_ref[...] = jnp.dot(
        tok_ref[...], rhs_ref[...], preferred_element_type=jnp.float32
    ).astype(out_ref.dtype)


def project(at, tokens, own, others):
    replicas, rows, width = own.shape
    tall, depth = tokens.shape
    far = others[0].shape[0]
    return pl.pallas_call(
        functools.partial(project_kernel, replicas),
        out_shape=jax.ShapeDtypeStruct((tall, width * replicas), jnp.bfloat16),
        grid_spec=pltpu.PrefetchScalarGridSpec(
            num_scalar_prefetch=1,
            grid=(replicas,),
            in_specs=[
                pl.BlockSpec((tall, depth), lambda k, at: (0, 0)),
                pl.BlockSpec((1, rows, width), lambda k, at: (k, 0, 0)),
            ]
            + [pl.BlockSpec((far, width), lambda k, at: (0, 0))] * replicas,
            out_specs=pl.BlockSpec((tall, width), lambda k, at: (0, at[0] ^ k)),
            scratch_shapes=[pltpu.VMEM((depth, width), jnp.bfloat16)],
        ),
        compiler_params=params(24),
    )(at, tokens, own, *others)


def swap(x, axis, flip):
    return lax.ppermute(x, axis, [(i, i ^ flip) for i in range(lax.axis_size(axis))])


def on_device(base, local, momentum, tokens):
    replicas, groups = lax.axis_size("rep"), lax.axis_size("fsdp")
    chips = replicas // 2
    width = base.shape[1] // replicas
    at = jnp.stack([lax.axis_index("rep"), lax.axis_index("fsdp")]).astype(jnp.int32)

    send = encode(at, base, local, 1, chips, width)
    recv = swap(send, "rep", 1)
    keep = encode(at, base, local, 0, chips, width)
    sums = chip_sum(keep, recv)
    parts = [swap(sums[j], "rep", 2 * j) for j in range(1, chips)]
    average, fresh = chunk_step(at, base, momentum, sums[0], parts, replicas)

    far = jnp.concatenate([swap(fresh, "fsdp", s) for s in range(1, groups)], axis=0)
    averages = [average] + [swap(average, "rep", 2 * j) for j in range(1, chips)]
    averages = [x for a in averages for x in (a, swap(a, "rep", 1))]
    new_base, new_momentum, own = outer(at, base, momentum, averages)

    others = [far] + [swap(far, "rep", 2 * j) for j in range(1, chips)]
    others = [x for a in others for x in (a, swap(a, "rep", 1))]
    projected = project(at, tokens, own, others)
    return new_base, new_momentum, projected


def solution(mesh):
    in_specs = (P("fsdp", None), P("rep", "fsdp", None), P("fsdp", None), P(("rep", "fsdp"), None))
    out_specs = (P("fsdp", None), P("fsdp", None), P(("rep", "fsdp"), None))
    return jax.shard_map(
        on_device, mesh=mesh, in_specs=in_specs, out_specs=out_specs, check_vma=False
    )
```

```python
import functools

import jax
import jax.numpy as jnp
from jax import lax
from jax.experimental import pallas as pl
from jax.experimental.pallas import tpu as pltpu
from jax.sharding import PartitionSpec as P

BLOCK = 128
MIB = 1 << 20

outer_lr = 0.7
outer_mu = 0.9

HBM = pl.BlockSpec(memory_space=pltpu.HBM)
VMEM = pl.BlockSpec(memory_space=pltpu.VMEM)


def params(mib=8):
    return pltpu.CompilerParams(vmem_limit_bytes=mib * MIB)


def columns(chunk, width):
    return pl.ds(pl.multiple_of(chunk * width, width), width)


def decoded_block(base, replica):
    delta = base - replica.astype(jnp.float32)
    scale = jnp.max(jnp.abs(delta), axis=1, keepdims=True) + 1e-06
    code = (delta / scale).astype(jnp.bfloat16)
    return (code.astype(jnp.float32) * scale).astype(jnp.bfloat16)


def encode_kernel(flip, base_hbm, local_hbm, out_ref, base_ref, local_ref, sems):
    chips, rows, width = out_ref.shape
    me = lax.axis_index("rep")
    copies = []
    for j in range(chips):
        cols = columns(me ^ (flip ^ (2 * j)), width)
        pair = (
            pltpu.make_async_copy(base_hbm.at[:, cols], base_ref.at[j], sems.at[0, j]),
            pltpu.make_async_copy(local_hbm.at[0, :, cols], local_ref.at[j], sems.at[1, j]),
        )
        for copy in pair:
            copy.start()
        copies.append(pair)
    for j in range(chips):
        for copy in copies[j]:
            copy.wait()
        for b in range(width // BLOCK):
            cols = slice(b * BLOCK, (b + 1) * BLOCK)
            out_ref[j, :, cols] = decoded_block(base_ref[j, :, cols], local_ref[j, :, cols])


def encode(base, local, flip, chips, width):
    rows = base.shape[0]
    return pl.pallas_call(
        functools.partial(encode_kernel, flip),
        out_shape=jax.ShapeDtypeStruct((chips, rows, width), jnp.bfloat16),
        in_specs=[HBM, HBM],
        out_specs=VMEM,
        scratch_shapes=[
            pltpu.VMEM((chips, rows, width), jnp.float32),
            pltpu.VMEM((chips, rows, width), jnp.bfloat16),
            pltpu.SemaphoreType.DMA((2, chips)),
        ],
        compiler_params=params(),
    )(base, local)


def chip_sum_kernel(keep_ref, recv_ref, *out_refs):
    for j, out_ref in enumerate(out_refs):
        total = keep_ref[j].astype(jnp.float32) + recv_ref[j].astype(jnp.float32)
        out_ref[...] = total.astype(out_ref.dtype)


def chip_sum(keep, recv):
    chips, rows, width = keep.shape
    return pl.pallas_call(
        chip_sum_kernel,
        out_shape=[
            jax.ShapeDtypeStruct((rows, width), jnp.float32 if j == 0 else jnp.bfloat16)
            for j in range(chips)
        ],
        compiler_params=params(),
    )(keep, recv)


def stepped(average, base, momentum):
    moved = outer_mu * momentum + average
    return base - outer_lr * (average + outer_mu * moved), moved


def chunk_step_kernel(replicas, base_ref, mom_ref, own_ref, *refs):
    parts, (avg_ref, fresh_ref) = refs[:-2], refs[-2:]
    cols = columns(lax.axis_index("rep"), own_ref.shape[1])
    total = own_ref[...]
    for part in parts:
        total = total + part[...].astype(jnp.float32)
    average = (total / replicas).astype(jnp.bfloat16)
    avg_ref[...] = average
    new_base, _ = stepped(average.astype(jnp.float32), base_ref[:, cols], mom_ref[:, cols])
    fresh_ref[...] = new_base.astype(jnp.bfloat16)


def chunk_step(base, momentum, own, parts, replicas):
    return pl.pallas_call(
        functools.partial(chunk_step_kernel, replicas),
        out_shape=[jax.ShapeDtypeStruct(own.shape, jnp.bfloat16)] * 2,
        compiler_params=params(),
    )(base, momentum, own, *parts)


def outer_kernel(replicas, base_ref, mom_ref, *refs):
    firsts, (new_base_hbm, new_mom_hbm, fresh_ref) = refs[:replicas], refs[replicas:-3]
    new_base_ref, new_mom_ref, sems = refs[-3:]
    rows, width = fresh_ref.shape[1:]
    me = lax.axis_index("rep")
    copies = []
    for k, first in enumerate(firsts):
        cols = columns(me ^ k, width)
        average = first[:rows, :].astype(jnp.float32)
        new_base, moved = stepped(average, base_ref[:, cols], mom_ref[:, cols])
        new_base_ref[k] = new_base
        new_mom_ref[k] = moved
        fresh_ref[k] = new_base.astype(jnp.bfloat16)
        for which, (ref, hbm) in enumerate(
            ((new_base_ref, new_base_hbm), (new_mom_ref, new_mom_hbm))
        ):
            copy = pltpu.make_async_copy(ref.at[k], hbm.at[:, cols], sems.at[which, k])
            copy.start()
            copies.append(copy)
    for copy in copies:
        copy.wait()


def outer(base, momentum, firsts, width):
    rows = base.shape[0]
    replicas = len(firsts)
    return pl.pallas_call(
        functools.partial(outer_kernel, replicas),
        out_shape=[
            jax.ShapeDtypeStruct(base.shape, jnp.float32),
            jax.ShapeDtypeStruct(base.shape, jnp.float32),
            jax.ShapeDtypeStruct((replicas, rows, width), jnp.bfloat16),
        ],
        out_specs=[HBM, HBM, VMEM],
        scratch_shapes=[
            pltpu.VMEM((replicas, rows, width), jnp.float32),
            pltpu.VMEM((replicas, rows, width), jnp.float32),
            pltpu.SemaphoreType.DMA((2, replicas)),
        ],
        compiler_params=params(),
    )(base, momentum, *firsts)


def project_kernel(places, near, tok_ref, own_ref, *refs):
    count = len(places)
    firsts, seconds = refs[:count], refs[count : 2 * count]
    out_hbm, rhs_ref, out_ref, sems = refs[-4:]
    rows, width = own_ref.shape[1:]
    me, here = lax.axis_index("rep"), lax.axis_index("fsdp")

    def at(s):
        return pl.ds(pl.multiple_of((here ^ s) * rows, rows), rows)

    copies = []
    for i, k in enumerate(places):
        rhs_ref[i, at(0), :] = own_ref[k]
        for s in range(1, near + 1):
            rhs_ref[i, at(s), :] = firsts[i][s * rows : (s + 1) * rows, :]
        for s in range(seconds[i].shape[0] // rows):
            rhs_ref[i, at(s + near + 1), :] = seconds[i][s * rows : (s + 1) * rows, :]
        out_ref[i] = jnp.dot(
            tok_ref[...], rhs_ref[i], preferred_element_type=jnp.float32
        ).astype(out_ref.dtype)
        copy = pltpu.make_async_copy(
            out_ref.at[i], out_hbm.at[:, columns(me ^ k, width)], sems.at[i]
        )
        copy.start()
        copies.append(copy)
    for copy in copies:
        copy.wait()


def project(out, tokens, own, firsts, seconds, places, near):
    replicas, rows, width = own.shape
    tall, depth = tokens.shape
    count = len(places)
    args = [tokens, own] + [firsts[k] for k in places] + [seconds[k] for k in places]
    specs = [VMEM] * len(args)
    alias = {}
    if out is not None:
        alias = {len(args): 0}
        args.append(out)
        specs.append(HBM)
    return pl.pallas_call(
        functools.partial(project_kernel, places, near),
        out_shape=jax.ShapeDtypeStruct((tall, width * replicas), jnp.bfloat16),
        in_specs=specs,
        out_specs=HBM,
        input_output_aliases=alias,
        scratch_shapes=[
            pltpu.VMEM((count, depth, width), jnp.bfloat16),
            pltpu.VMEM((count, tall, width), jnp.bfloat16),
            pltpu.SemaphoreType.DMA((count,)),
        ],
        compiler_params=params(16),
    )(*args)


def swap(x, axis, flip):
    return lax.ppermute(x, axis, [(i, i ^ flip) for i in range(lax.axis_size(axis))])


def spread(own, chips):
    held = [own] + [swap(own, "rep", 2 * j) for j in range(1, chips)]
    return [x for a in held for x in (a, swap(a, "rep", 1))]


def on_device(base, local, momentum, tokens):
    replicas, groups = lax.axis_size("rep"), lax.axis_size("fsdp")
    chips = replicas // 2
    near = groups // 4
    width = base.shape[1] // replicas

    send = encode(base, local, 1, chips, width)
    recv = swap(send, "rep", 1)
    keep = encode(base, local, 0, chips, width)
    sums = chip_sum(keep, recv)
    parts = [swap(sums[j], "rep", 2 * j) for j in range(1, chips)]
    average, fresh = chunk_step(base, momentum, sums[0], parts, replicas)

    far = [swap(fresh, "fsdp", s) for s in range(1, groups)]
    firsts = spread(jnp.concatenate([average] + far[:near], axis=0), chips)
    seconds = spread(jnp.concatenate(far[near:], axis=0), chips)

    new_base, new_momentum, own = outer(base, momentum, firsts, width)
    projected = None
    for j in [0] + list(range(chips - 1, 0, -1)):
        projected = project(projected, tokens, own, firsts, seconds, (2 * j, 2 * j + 1), near)
    return new_base, new_momentum, projected


def solution(mesh):
    in_specs = (P("fsdp", None), P("rep", "fsdp", None), P("fsdp", None), P(("rep", "fsdp"), None))
    out_specs = (P("fsdp", None), P("fsdp", None), P(("rep", "fsdp"), None))
    return jax.shard_map(
        on_device, mesh=mesh, in_specs=in_specs, out_specs=out_specs, check_vma=False
    )
```

```python
import functools

import jax
import jax.numpy as jnp
from jax import lax
from jax.experimental import pallas as pl
from jax.experimental.pallas import tpu as pltpu
from jax.sharding import PartitionSpec as P

BLOCK = 128
MIB = 1 << 20

outer_lr = 0.7
outer_mu = 0.9

HBM = pl.BlockSpec(memory_space=pltpu.HBM)
VMEM = pl.BlockSpec(memory_space=pltpu.VMEM)
COST = pl.CostEstimate(flops=1 << 34, transcendentals=0, bytes_accessed=1 << 26)


def params(mib=8):
    return pltpu.CompilerParams(vmem_limit_bytes=mib * MIB)


def columns(chunk, width):
    return pl.ds(pl.multiple_of(chunk * width, width), width)


def decoded_block(base, replica):
    delta = base - replica.astype(jnp.float32)
    scale = jnp.max(jnp.abs(delta), axis=1, keepdims=True) + 1e-06
    code = (delta / scale).astype(jnp.bfloat16)
    return (code.astype(jnp.float32) * scale).astype(jnp.bfloat16)


def encode_kernel(flip, base_hbm, local_hbm, out_ref, base_ref, local_ref, sems):
    chips, rows, width = out_ref.shape
    me = lax.axis_index("rep")
    copies = []
    for j in range(chips):
        cols = columns(me ^ (flip ^ (2 * j)), width)
        pair = (
            pltpu.make_async_copy(base_hbm.at[:, cols], base_ref.at[j], sems.at[0, j]),
            pltpu.make_async_copy(local_hbm.at[0, :, cols], local_ref.at[j], sems.at[1, j]),
        )
        for copy in pair:
            copy.start()
        copies.append(pair)
    for j in range(chips):
        for copy in copies[j]:
            copy.wait()
        for b in range(width // BLOCK):
            cols = slice(b * BLOCK, (b + 1) * BLOCK)
            out_ref[j, :, cols] = decoded_block(base_ref[j, :, cols], local_ref[j, :, cols])


def encode(base, local, flip, chips, width):
    rows = base.shape[0]
    base = pltpu.with_memory_space_constraint(base, pltpu.HBM)
    local = pltpu.with_memory_space_constraint(local, pltpu.HBM)
    return pl.pallas_call(
        functools.partial(encode_kernel, flip),
        out_shape=jax.ShapeDtypeStruct((chips, rows, width), jnp.bfloat16),
        in_specs=[HBM, HBM],
        out_specs=VMEM,
        scratch_shapes=[
            pltpu.VMEM((chips, rows, width), jnp.float32),
            pltpu.VMEM((chips, rows, width), jnp.bfloat16),
            pltpu.SemaphoreType.DMA((2, chips)),
        ],
        cost_estimate=COST,
        compiler_params=params(),
    )(base, local)


def chip_sum_kernel(keep_ref, recv_ref, *out_refs):
    for j, out_ref in enumerate(out_refs):
        total = keep_ref[j].astype(jnp.float32) + recv_ref[j].astype(jnp.float32)
        out_ref[...] = total.astype(out_ref.dtype)


def chip_sum(keep, recv):
    chips, rows, width = keep.shape
    return pl.pallas_call(
        chip_sum_kernel,
        out_shape=[
            jax.ShapeDtypeStruct((rows, width), jnp.float32 if j == 0 else jnp.bfloat16)
            for j in range(chips)
        ],
        cost_estimate=COST,
        compiler_params=params(),
    )(keep, recv)


def stepped(average, base, momentum):
    moved = outer_mu * momentum + average
    return base - outer_lr * (average + outer_mu * moved), moved


def chunk_step_kernel(replicas, base_ref, mom_ref, own_ref, *refs):
    parts, (avg_ref, fresh_ref) = refs[:-2], refs[-2:]
    cols = columns(lax.axis_index("rep"), own_ref.shape[1])
    total = own_ref[...]
    for part in parts:
        total = total + part[...].astype(jnp.float32)
    average = (total / replicas).astype(jnp.bfloat16)
    avg_ref[...] = average
    new_base, _ = stepped(average.astype(jnp.float32), base_ref[:, cols], mom_ref[:, cols])
    fresh_ref[...] = new_base.astype(jnp.bfloat16)


def chunk_step(base, momentum, own, parts, replicas):
    return pl.pallas_call(
        functools.partial(chunk_step_kernel, replicas),
        out_shape=[jax.ShapeDtypeStruct(own.shape, jnp.bfloat16)] * 2,
        cost_estimate=COST,
        compiler_params=params(),
    )(base, momentum, own, *parts)


def outer_kernel(base_ref, mom_ref, *refs):
    firsts, (new_base_ref, new_mom_ref, fresh_ref) = refs[:-3], refs[-3:]
    rows, width = fresh_ref.shape[1:]
    me = lax.axis_index("rep")
    for k, first in enumerate(firsts):
        cols = columns(me ^ k, width)
        average = first[:rows, :].astype(jnp.float32)
        new_base, moved = stepped(average, base_ref[:, cols], mom_ref[:, cols])
        new_base_ref[:, cols] = new_base
        new_mom_ref[:, cols] = moved
        fresh_ref[k] = new_base.astype(jnp.bfloat16)


def outer(base, momentum, firsts, width):
    rows = base.shape[0]
    replicas = len(firsts)
    return pl.pallas_call(
        outer_kernel,
        out_shape=[
            jax.ShapeDtypeStruct(base.shape, jnp.float32),
            jax.ShapeDtypeStruct(base.shape, jnp.float32),
            jax.ShapeDtypeStruct((replicas, rows, width), jnp.bfloat16),
        ],
        cost_estimate=COST,
        compiler_params=params(),
    )(base, momentum, *firsts)


def stack(rhs_ref, i, own, first, second, near):
    rows = own.shape[0]
    here = lax.axis_index("fsdp")
    pieces = [own[...]]
    pieces += [first[s * rows : (s + 1) * rows, :] for s in range(1, near + 1)]
    pieces += [second[s * rows : (s + 1) * rows, :] for s in range(second.shape[0] // rows)]
    for s, piece in enumerate(pieces):
        rhs_ref[i, pl.ds(pl.multiple_of((here ^ s) * rows, rows), rows), :] = piece


def stack_kernel(places, near, own_ref, *refs):
    count = len(places)
    out_ref, rhs_ref, sems = refs[-3:]
    copies = []
    for i, k in enumerate(places):
        stack(rhs_ref, i, own_ref.at[k], refs[i], refs[count + i], near)
        copies.append(pltpu.make_async_copy(rhs_ref.at[i], out_ref.at[k], sems.at[i]))
        copies[-1].start()
    for copy in copies:
        copy.wait()


def stacked(rhs, depth, own, firsts, seconds, places, near):
    replicas, rows, width = own.shape
    count = len(places)
    args = [own] + [firsts[k] for k in places] + [seconds[k] for k in places]
    specs = [VMEM] * len(args)
    alias = {}
    if rhs is not None:
        alias = {len(args): 0}
        args.append(rhs)
        specs.append(pl.BlockSpec(memory_space=pl.ANY))
    return pl.pallas_call(
        functools.partial(stack_kernel, places, near),
        out_shape=jax.ShapeDtypeStruct((replicas, depth, width), jnp.bfloat16),
        in_specs=specs,
        out_specs=pl.BlockSpec(memory_space=pl.ANY),
        input_output_aliases=alias,
        scratch_shapes=[
            pltpu.VMEM((count, depth, width), jnp.bfloat16),
            pltpu.SemaphoreType.DMA((count,)),
        ],
        cost_estimate=COST,
        compiler_params=params(),
    )(*args)


def project_kernel(places, near, tok_ref, own_ref, base_ref, mom_ref, *refs):
    count = len(places)
    replicas, rows, width = own_ref.shape
    firsts, seconds, stacked_ref = refs[:count], refs[count : 2 * count], refs[2 * count]
    out_hbm, new_base_hbm, new_mom_hbm, rhs_ref, out_ref, sems = refs[-6:]
    me = lax.axis_index("rep")
    copies = [
        pltpu.make_async_copy(base_ref, new_base_hbm, sems.at[replicas]),
        pltpu.make_async_copy(mom_ref, new_mom_hbm, sems.at[replicas + 1]),
    ]
    for copy in copies:
        copy.start()

    def emit(k, rhs):
        out_ref[k] = jnp.dot(tok_ref[...], rhs, preferred_element_type=jnp.float32).astype(
            out_ref.dtype
        )
        copy = pltpu.make_async_copy(
            out_ref.at[k], out_hbm.at[:, columns(me ^ k, width)], sems.at[k]
        )
        copy.start()
        copies.append(copy)

    for k in range(replicas):
        if k not in places:
            emit(k, stacked_ref[k])
    for i, k in enumerate(places):
        stack(rhs_ref, i, own_ref.at[k], firsts[i], seconds[i], near)
        emit(k, rhs_ref[i])
    for copy in copies:
        copy.wait()


def project(rhs, tokens, own, new_base, new_mom, firsts, seconds, places, near):
    replicas, rows, width = own.shape
    tall, depth = tokens.shape
    count = len(places)
    args = [tokens, own, new_base, new_mom]
    args += [firsts[k] for k in places] + [seconds[k] for k in places] + [rhs]
    return pl.pallas_call(
        functools.partial(project_kernel, places, near),
        out_shape=[
            jax.ShapeDtypeStruct((tall, width * replicas), jnp.bfloat16),
            jax.ShapeDtypeStruct(new_base.shape, jnp.float32),
            jax.ShapeDtypeStruct(new_base.shape, jnp.float32),
        ],
        out_specs=[HBM, HBM, HBM],
        scratch_shapes=[
            pltpu.VMEM((count, depth, width), jnp.bfloat16),
            pltpu.VMEM((replicas, tall, width), jnp.bfloat16),
            pltpu.SemaphoreType.DMA((replicas + 2,)),
        ],
        cost_estimate=COST,
        compiler_params=params(),
    )(*args)


def swap(x, axis, flip):
    return lax.ppermute(x, axis, [(i, i ^ flip) for i in range(lax.axis_size(axis))])


def join_kernel(*refs):
    at = 0
    for ref in refs[:-1]:
        refs[-1][at : at + ref.shape[0], :] = ref[...]
        at += ref.shape[0]


def join(xs):
    return pl.pallas_call(
        join_kernel,
        out_shape=jax.ShapeDtypeStruct((sum(x.shape[0] for x in xs),) + xs[0].shape[1:], xs[0].dtype),
        cost_estimate=COST,
        compiler_params=params(),
    )(*xs)


def on_device(base, local, momentum, tokens):
    replicas, groups = lax.axis_size("rep"), lax.axis_size("fsdp")
    chips = replicas // 2
    near = groups // 4
    width = base.shape[1] // replicas

    send = encode(base, local, 1, chips, width)
    recv = swap(send, "rep", 1)
    keep = encode(base, local, 0, chips, width)
    sums = chip_sum(keep, recv)
    parts = [swap(sums[j], "rep", 2 * j) for j in range(1, chips)]
    average, fresh = chunk_step(base, momentum, sums[0], parts, replicas)

    far = [swap(fresh, "fsdp", s) for s in range(1, groups)]
    first = join([average] + far[:near])
    second = join(far[near:])
    firsts = [first] + [swap(first, "rep", 2 * j) for j in range(1, chips)]
    seconds = [second] + [swap(second, "rep", 2 * j) for j in range(1, chips)]
    last = swap(second, "rep", 1)
    firsts = [x for a in firsts for x in (a, swap(a, "rep", 1))]
    new_base, new_momentum, own = outer(base, momentum, firsts, width)
    lasts = [last] + [swap(a, "rep", 1) for a in seconds[:0:-1]][::-1]
    seconds = [x for pair in zip(seconds, lasts) for x in pair]

    order = [(2 * j, 2 * j + 1) for j in [0] + list(range(chips - 1, 0, -1))]
    rhs = None
    for places in order[:-1]:
        rhs = stacked(rhs, tokens.shape[1], own, firsts, seconds, places, near)
    projected, new_base, new_momentum = project(
        rhs, tokens, own, new_base, new_momentum, firsts, seconds, order[-1], near
    )
    return new_base, new_momentum, projected


def solution(mesh):
    in_specs = (P("fsdp", None), P("rep", "fsdp", None), P("fsdp", None), P(("rep", "fsdp"), None))
    out_specs = (P("fsdp", None), P("fsdp", None), P(("rep", "fsdp"), None))
    return jax.shard_map(
        on_device, mesh=mesh, in_specs=in_specs, out_specs=out_specs, check_vma=False
    )
```

```python
import functools

import jax
import jax.numpy as jnp
from jax import lax
from jax.experimental import pallas as pl
from jax.experimental.pallas import tpu as pltpu
from jax.sharding import PartitionSpec as P

BLOCK = 128
MIB = 1 << 20

outer_lr = 0.7
outer_mu = 0.9

HBM = pl.BlockSpec(memory_space=pltpu.HBM)
VMEM = pl.BlockSpec(memory_space=pltpu.VMEM)
COST = pl.CostEstimate(flops=1 << 34, transcendentals=0, bytes_accessed=1 << 26)


def params(mib=8):
    return pltpu.CompilerParams(vmem_limit_bytes=mib * MIB)


def columns(chunk, width):
    return pl.ds(pl.multiple_of(chunk * width, width), width)


def decoded_block(base, replica):
    delta = base - replica.astype(jnp.float32)
    scale = jnp.max(jnp.abs(delta), axis=1, keepdims=True) + 1e-06
    code = (delta / scale).astype(jnp.bfloat16)
    return (code.astype(jnp.float32) * scale).astype(jnp.bfloat16)


def encode_kernel(flip, base_hbm, local_hbm, *refs):
    *staged, tok_ref, base_ref, local_ref, sems = refs
    out_ref = staged[1] if staged else tok_ref
    chips, rows, width = out_ref.shape
    me = lax.axis_index("rep")
    copies = []
    if staged:
        stage = pltpu.make_async_copy(staged[0], tok_ref, sems.at[2, 0])
    for j in range(chips):
        cols = columns(me ^ (flip ^ (2 * j)), width)
        pair = (
            pltpu.make_async_copy(base_hbm.at[:, cols], base_ref.at[j], sems.at[0, j]),
            pltpu.make_async_copy(local_hbm.at[0, :, cols], local_ref.at[j], sems.at[1, j]),
        )
        for copy in pair:
            copy.start()
        copies.append(pair)
    if staged:
        stage.start()
    for j in range(chips):
        for copy in copies[j]:
            copy.wait()
        for b in range(width // BLOCK):
            cols = slice(b * BLOCK, (b + 1) * BLOCK)
            out_ref[j, :, cols] = decoded_block(base_ref[j, :, cols], local_ref[j, :, cols])
    if staged:
        stage.wait()


def encode(base, local, flip, chips, width, tokens=None):
    rows = base.shape[0]
    base = pltpu.with_memory_space_constraint(base, pltpu.HBM)
    local = pltpu.with_memory_space_constraint(local, pltpu.HBM)
    args, shapes = [base, local], [jax.ShapeDtypeStruct((chips, rows, width), jnp.bfloat16)]
    if tokens is not None:
        args.append(pltpu.with_memory_space_constraint(tokens, pltpu.HBM))
        shapes.append(jax.ShapeDtypeStruct(tokens.shape, tokens.dtype))
    return pl.pallas_call(
        functools.partial(encode_kernel, flip),
        out_shape=shapes,
        in_specs=[HBM] * len(args),
        out_specs=[VMEM] * len(shapes),
        scratch_shapes=[
            pltpu.VMEM((chips, rows, width), jnp.float32),
            pltpu.VMEM((chips, rows, width), jnp.bfloat16),
            pltpu.SemaphoreType.DMA((3, chips)),
        ],
        cost_estimate=COST,
        compiler_params=params(),
    )(*args)


def chip_sum_kernel(keep_ref, recv_ref, *out_refs):
    for j, out_ref in enumerate(out_refs):
        total = keep_ref[j].astype(jnp.float32) + recv_ref[j].astype(jnp.float32)
        out_ref[...] = total.astype(out_ref.dtype)


def chip_sum(keep, recv):
    chips, rows, width = keep.shape
    return pl.pallas_call(
        chip_sum_kernel,
        out_shape=[
            jax.ShapeDtypeStruct((rows, width), jnp.float32 if j == 0 else jnp.bfloat16)
            for j in range(chips)
        ],
        cost_estimate=COST,
        compiler_params=params(),
    )(keep, recv)


def stepped(average, base, momentum):
    moved = outer_mu * momentum + average
    return base - outer_lr * (average + outer_mu * moved), moved


def chunk_step_kernel(replicas, base_ref, mom_ref, own_ref, *refs):
    parts, (avg_ref, fresh_ref) = refs[:-2], refs[-2:]
    cols = columns(lax.axis_index("rep"), own_ref.shape[1])
    total = own_ref[...]
    for part in parts:
        total = total + part[...].astype(jnp.float32)
    average = (total / replicas).astype(jnp.bfloat16)
    avg_ref[...] = average
    new_base, _ = stepped(average.astype(jnp.float32), base_ref[:, cols], mom_ref[:, cols])
    fresh_ref[...] = new_base.astype(jnp.bfloat16)


def chunk_step(base, momentum, own, parts, replicas):
    return pl.pallas_call(
        functools.partial(chunk_step_kernel, replicas),
        out_shape=[jax.ShapeDtypeStruct(own.shape, jnp.bfloat16)] * 2,
        cost_estimate=COST,
        compiler_params=params(),
    )(base, momentum, own, *parts)


def gather_slots(slots):
    arrays, where = [], []
    for array, place in slots:
        known = [i for i, other in enumerate(arrays) if other is array]
        if not known:
            arrays.append(array)
        where.append((known[0] if known else len(arrays) - 1, place))
    return arrays, where


def at_slot(refs, slot):
    number, place = slot
    return refs[number] if place is None else refs[number].at[place]


def outer_kernel(where, base_ref, mom_ref, *refs):
    holders, (new_base_ref, new_mom_ref, fresh_ref) = refs[:-3], refs[-3:]
    rows, width = fresh_ref.shape[1:]
    me = lax.axis_index("rep")
    for k, slot in enumerate(where):
        cols = columns(me ^ k, width)
        average = at_slot(holders, slot)[:rows, :].astype(jnp.float32)
        new_base, moved = stepped(average, base_ref[:, cols], mom_ref[:, cols])
        new_base_ref[:, cols] = new_base
        new_mom_ref[:, cols] = moved
        fresh_ref[k] = new_base.astype(jnp.bfloat16)


def outer(base, momentum, firsts, width):
    rows = base.shape[0]
    arrays, where = gather_slots(firsts)
    return pl.pallas_call(
        functools.partial(outer_kernel, where),
        out_shape=[
            jax.ShapeDtypeStruct(base.shape, jnp.float32),
            jax.ShapeDtypeStruct(base.shape, jnp.float32),
            jax.ShapeDtypeStruct((len(firsts), rows, width), jnp.bfloat16),
        ],
        cost_estimate=COST,
        compiler_params=params(),
    )(base, momentum, *arrays)


def stack(rhs_ref, i, own, first, second, near):
    rows = own.shape[0]
    here = lax.axis_index("fsdp")
    pieces = [own[...]]
    pieces += [first[s * rows : (s + 1) * rows, :] for s in range(1, near + 1)]
    pieces += [second[s * rows : (s + 1) * rows, :] for s in range(second.shape[0] // rows)]
    for s, piece in enumerate(pieces):
        rhs_ref[i, pl.ds(pl.multiple_of((here ^ s) * rows, rows), rows), :] = piece


def stack_kernel(places, near, where, own_ref, *refs):
    count = len(places)
    out_ref, rhs_ref, sems = refs[-3:]
    copies = []
    for i, k in enumerate(places):
        first, second = at_slot(refs, where[i]), at_slot(refs, where[count + i])
        stack(rhs_ref, i, own_ref.at[k], first, second, near)
        copies.append(pltpu.make_async_copy(rhs_ref.at[i], out_ref.at[k], sems.at[i]))
        copies[-1].start()
    for copy in copies:
        copy.wait()


def stacked(rhs, depth, own, firsts, seconds, places, near):
    replicas, rows, width = own.shape
    count = len(places)
    arrays, where = gather_slots([firsts[k] for k in places] + [seconds[k] for k in places])
    args = [own] + arrays
    specs = [VMEM] * len(args)
    alias = {}
    if rhs is not None:
        alias = {len(args): 0}
        args.append(rhs)
        specs.append(pl.BlockSpec(memory_space=pl.ANY))
    return pl.pallas_call(
        functools.partial(stack_kernel, places, near, where),
        out_shape=jax.ShapeDtypeStruct((replicas, depth, width), jnp.bfloat16),
        in_specs=specs,
        out_specs=pl.BlockSpec(memory_space=pl.ANY),
        input_output_aliases=alias,
        scratch_shapes=[
            pltpu.VMEM((count, depth, width), jnp.bfloat16),
            pltpu.SemaphoreType.DMA((count,)),
        ],
        cost_estimate=COST,
        compiler_params=params(),
    )(*args)


def project_kernel(places, near, where, tok_ref, own_ref, base_ref, mom_ref, *refs):
    count = len(places)
    replicas, rows, width = own_ref.shape
    out_hbm, new_base_hbm, new_mom_hbm, rhs_ref, out_ref, sems = refs[-6:]
    stacked_ref = refs[-7]
    me = lax.axis_index("rep")
    copies = [
        pltpu.make_async_copy(base_ref, new_base_hbm, sems.at[replicas]),
        pltpu.make_async_copy(mom_ref, new_mom_hbm, sems.at[replicas + 1]),
    ]
    for copy in copies:
        copy.start()

    def emit(k, rhs):
        out_ref[k] = jnp.dot(tok_ref[...], rhs, preferred_element_type=jnp.float32).astype(
            out_ref.dtype
        )
        copy = pltpu.make_async_copy(
            out_ref.at[k], out_hbm.at[:, columns(me ^ k, width)], sems.at[k]
        )
        copy.start()
        copies.append(copy)

    for k in range(replicas):
        if k not in places:
            emit(k, stacked_ref[k])
    for i, k in enumerate(places):
        first, second = at_slot(refs, where[i]), at_slot(refs, where[count + i])
        stack(rhs_ref, i, own_ref.at[k], first, second, near)
        emit(k, rhs_ref[i])
    for copy in copies:
        copy.wait()


def project(rhs, tokens, own, new_base, new_mom, firsts, seconds, places, near):
    replicas, rows, width = own.shape
    tall, depth = tokens.shape
    count = len(places)
    arrays, where = gather_slots([firsts[k] for k in places] + [seconds[k] for k in places])
    args = [tokens, own, new_base, new_mom] + arrays
    if rhs is not None:
        args.append(rhs)
    return pl.pallas_call(
        functools.partial(project_kernel, places, near, where),
        out_shape=[
            jax.ShapeDtypeStruct((tall, width * replicas), jnp.bfloat16),
            jax.ShapeDtypeStruct(new_base.shape, jnp.float32),
            jax.ShapeDtypeStruct(new_base.shape, jnp.float32),
        ],
        out_specs=[HBM, HBM, HBM],
        scratch_shapes=[
            pltpu.VMEM((count, depth, width), jnp.bfloat16),
            pltpu.VMEM((replicas, tall, width), jnp.bfloat16),
            pltpu.SemaphoreType.DMA((replicas + 2,)),
        ],
        cost_estimate=COST,
        compiler_params=params(),
    )(*args)


def swap(x, axis, flip):
    return lax.ppermute(x, axis, [(i, i ^ flip) for i in range(lax.axis_size(axis))])


def join_kernel(*refs):
    at = 0
    for ref in refs[:-1]:
        refs[-1][at : at + ref.shape[0], :] = ref[...]
        at += ref.shape[0]


def join(xs):
    return pl.pallas_call(
        join_kernel,
        out_shape=jax.ShapeDtypeStruct((sum(x.shape[0] for x in xs),) + xs[0].shape[1:], xs[0].dtype),
        cost_estimate=COST,
        compiler_params=params(),
    )(*xs)


def pile_kernel(*refs):
    for i, ref in enumerate(refs[:-1]):
        refs[-1][i] = ref[...]


def pile(xs):
    return pl.pallas_call(
        pile_kernel,
        out_shape=jax.ShapeDtypeStruct((len(xs),) + xs[0].shape, xs[0].dtype),
        cost_estimate=COST,
        compiler_params=params(),
    )(*xs)


def share(held, groups):
    slots = {2 * j: (x, None) for j, x in enumerate(held)}
    for group in groups:
        if len(group) == 1:
            slots[2 * group[0] + 1] = (swap(held[group[0]], "rep", 1), None)
        else:
            got = swap(pile([held[j] for j in group]), "rep", 1)
            for i, j in enumerate(group):
                slots[2 * j + 1] = (got, i)
    return [slots[k] for k in range(2 * len(held))]


def after(x, *others):
    return lax.optimization_barrier((x,) + others)[0]


def on_device(base, local, momentum, tokens):
    replicas, groups = lax.axis_size("rep"), lax.axis_size("fsdp")
    chips = replicas // 2
    near = groups // 4
    width = base.shape[1] // replicas

    (send,) = encode(base, local, 1, chips, width)
    recv = swap(send, "rep", 1)
    keep, tokens = encode(base, local, 0, chips, width, tokens)
    sums = chip_sum(keep, recv)
    parts = [swap(sums[j], "rep", 2 * j) for j in range(1, chips)]
    average, fresh = chunk_step(base, momentum, sums[0], parts, replicas)

    far = [swap(fresh, "fsdp", s) for s in range(1, groups)]
    first = join([average] + far[:near])
    second = join(far[near:])
    firsts = [first] + [swap(first, "rep", 2 * j) for j in range(1, chips)]
    seconds = [second] + [swap(second, "rep", 2 * j) for j in range(1, chips)]
    firsts = [first] + [after(x, second) for x in firsts[1:]]
    firsts = share(firsts, [range(chips)])
    new_base, new_momentum, own = outer(base, momentum, firsts, width)
    seconds = share(seconds, [(0, chips - 1)] + [(j,) for j in range(chips - 2, 0, -1)])

    order = [(2 * j, 2 * j + 1) for j in [0] + list(range(chips - 1, 0, -1))]
    rhs = None
    for places in order[:-1]:
        rhs = stacked(rhs, tokens.shape[1], own, firsts, seconds, places, near)
    projected, new_base, new_momentum = project(
        rhs, tokens, own, new_base, new_momentum, firsts, seconds, order[-1], near
    )
    return new_base, new_momentum, projected


def solution(mesh):
    in_specs = (P("fsdp", None), P("rep", "fsdp", None), P("fsdp", None), P(("rep", "fsdp"), None))
    out_specs = (P("fsdp", None), P("fsdp", None), P(("rep", "fsdp"), None))
    return jax.shard_map(
        on_device, mesh=mesh, in_specs=in_specs, out_specs=out_specs, check_vma=False
    )
```

```python
import functools

import jax
import jax.numpy as jnp
from jax import lax
from jax.experimental import pallas as pl
from jax.experimental.pallas import tpu as pltpu
from jax.sharding import PartitionSpec as P

BLOCK = 128
MIB = 1 << 20

outer_lr = 0.7
outer_mu = 0.9

HBM = pl.BlockSpec(memory_space=pltpu.HBM)
VMEM = pl.BlockSpec(memory_space=pltpu.VMEM)
COST = pl.CostEstimate(flops=1 << 34, transcendentals=0, bytes_accessed=1 << 26)


def params(mib=8):
    return pltpu.CompilerParams(vmem_limit_bytes=mib * MIB)


def columns(rep, width, replicas):
    chunk = lax.rem(rep, 2) * (replicas // 2) + lax.div(rep, 2)
    return pl.ds(pl.multiple_of(chunk * width, width), width)


def decoded_block(base, replica):
    delta = base - replica.astype(jnp.float32)
    scale = jnp.max(jnp.abs(delta), axis=1, keepdims=True) + 1e-06
    code = (delta / scale).astype(jnp.bfloat16)
    return (code.astype(jnp.float32) * scale).astype(jnp.bfloat16)


def encode_kernel(flip, base_hbm, local_hbm, *refs):
    *staged, tok_ref, base_ref, local_ref, sems = refs
    out_ref = staged[1] if staged else tok_ref
    chips, rows, width = out_ref.shape
    pieces = sems.shape[1]
    me = lax.axis_index("rep")
    core, chip = lax.rem(me ^ flip, 2), lax.div(me, 2)
    piece = chips * width // pieces
    copies = []
    if staged:
        stage = pltpu.make_async_copy(staged[0], tok_ref, sems.at[2, 0])
    for p in range(pieces):
        here = slice(p * piece, (p + 1) * piece)
        there = pl.ds(pl.multiple_of((core * pieces + p) * piece, piece), piece)
        pair = (
            pltpu.make_async_copy(base_hbm.at[:, there], base_ref.at[:, here], sems.at[0, p]),
            pltpu.make_async_copy(local_hbm.at[0, :, there], local_ref.at[:, here], sems.at[1, p]),
        )
        for copy in pair:
            copy.start()
        copies.append(pair)
    if staged:
        stage.start()
    for p in range(pieces):
        for copy in copies[p]:
            copy.wait()
        for c in range(p * chips // pieces, (p + 1) * chips // pieces):
            for b in range(width // BLOCK):
                cols = slice(c * width + b * BLOCK, c * width + (b + 1) * BLOCK)
                out_ref[chip ^ c, :, b * BLOCK : (b + 1) * BLOCK] = decoded_block(
                    base_ref[:, cols], local_ref[:, cols]
                )
    if staged:
        stage.wait()


def encode(base, local, flip, chips, width, tokens=None):
    rows = base.shape[0]
    base = pltpu.with_memory_space_constraint(base, pltpu.HBM)
    local = pltpu.with_memory_space_constraint(local, pltpu.HBM)
    args, shapes = [base, local], [jax.ShapeDtypeStruct((chips, rows, width), jnp.bfloat16)]
    if tokens is not None:
        args.append(pltpu.with_memory_space_constraint(tokens, pltpu.HBM))
        shapes.append(jax.ShapeDtypeStruct(tokens.shape, tokens.dtype))
    return pl.pallas_call(
        functools.partial(encode_kernel, flip),
        out_shape=shapes,
        in_specs=[HBM] * len(args),
        out_specs=[VMEM] * len(shapes),
        scratch_shapes=[
            pltpu.VMEM((rows, chips * width), jnp.float32),
            pltpu.VMEM((rows, chips * width), jnp.bfloat16),
            pltpu.SemaphoreType.DMA((3, 2)),
        ],
        cost_estimate=COST,
        compiler_params=params(),
    )(*args)


def chip_sum_kernel(keep_ref, recv_ref, *out_refs):
    for j, out_ref in enumerate(out_refs):
        total = keep_ref[j].astype(jnp.float32) + recv_ref[j].astype(jnp.float32)
        out_ref[...] = total.astype(out_ref.dtype)


def chip_sum(keep, recv):
    chips, rows, width = keep.shape
    return pl.pallas_call(
        chip_sum_kernel,
        out_shape=[
            jax.ShapeDtypeStruct((rows, width), jnp.float32 if j == 0 else jnp.bfloat16)
            for j in range(chips)
        ],
        cost_estimate=COST,
        compiler_params=params(),
    )(keep, recv)


def stepped(average, base, momentum):
    moved = outer_mu * momentum + average
    return base - outer_lr * (average + outer_mu * moved), moved


def chunk_step_kernel(replicas, base_ref, mom_ref, own_ref, *refs):
    parts, (avg_ref, fresh_ref) = refs[:-2], refs[-2:]
    cols = columns(lax.axis_index("rep"), own_ref.shape[1], replicas)
    total = own_ref[...]
    for part in parts:
        total = total + part[...].astype(jnp.float32)
    average = (total / replicas).astype(jnp.bfloat16)
    avg_ref[...] = average
    new_base, _ = stepped(average.astype(jnp.float32), base_ref[:, cols], mom_ref[:, cols])
    fresh_ref[...] = new_base.astype(jnp.bfloat16)


def chunk_step(base, momentum, own, parts, replicas):
    return pl.pallas_call(
        functools.partial(chunk_step_kernel, replicas),
        out_shape=[jax.ShapeDtypeStruct(own.shape, jnp.bfloat16)] * 2,
        cost_estimate=COST,
        compiler_params=params(),
    )(base, momentum, own, *parts)


def gather_slots(slots):
    arrays, where = [], []
    for array, place in slots:
        known = [i for i, other in enumerate(arrays) if other is array]
        if not known:
            arrays.append(array)
        where.append((known[0] if known else len(arrays) - 1, place))
    return arrays, where


def at_slot(refs, slot):
    number, place = slot
    return refs[number] if place is None else refs[number].at[place]


def outer_kernel(where, base_ref, mom_ref, *refs):
    holders, (new_base_ref, new_mom_ref, fresh_ref) = refs[:-3], refs[-3:]
    rows, width = fresh_ref.shape[1:]
    me = lax.axis_index("rep")
    for k, slot in enumerate(where):
        cols = columns(me ^ k, width, len(where))
        average = at_slot(holders, slot)[:rows, :].astype(jnp.float32)
        new_base, moved = stepped(average, base_ref[:, cols], mom_ref[:, cols])
        new_base_ref[:, cols] = new_base
        new_mom_ref[:, cols] = moved
        fresh_ref[k] = new_base.astype(jnp.bfloat16)


def outer(base, momentum, firsts, width):
    rows = base.shape[0]
    arrays, where = gather_slots(firsts)
    return pl.pallas_call(
        functools.partial(outer_kernel, where),
        out_shape=[
            jax.ShapeDtypeStruct(base.shape, jnp.float32),
            jax.ShapeDtypeStruct(base.shape, jnp.float32),
            jax.ShapeDtypeStruct((len(firsts), rows, width), jnp.bfloat16),
        ],
        cost_estimate=COST,
        compiler_params=params(),
    )(base, momentum, *arrays)


def stack(rhs_ref, i, own, first, second, near):
    rows = own.shape[0]
    here = lax.axis_index("fsdp")
    pieces = [own[...]]
    pieces += [first[s * rows : (s + 1) * rows, :] for s in range(1, near + 1)]
    pieces += [second[s * rows : (s + 1) * rows, :] for s in range(second.shape[0] // rows)]
    for s, piece in enumerate(pieces):
        rhs_ref[i, pl.ds(pl.multiple_of((here ^ s) * rows, rows), rows), :] = piece


def stack_kernel(places, near, where, own_ref, *refs):
    count = len(places)
    out_ref, rhs_ref, sems = refs[-3:]
    copies = []
    for i, k in enumerate(places):
        first, second = at_slot(refs, where[i]), at_slot(refs, where[count + i])
        stack(rhs_ref, i, own_ref.at[k], first, second, near)
        copies.append(pltpu.make_async_copy(rhs_ref.at[i], out_ref.at[k], sems.at[i]))
        copies[-1].start()
    for copy in copies:
        copy.wait()


def stacked(rhs, depth, own, firsts, seconds, places, near):
    replicas, rows, width = own.shape
    count = len(places)
    arrays, where = gather_slots([firsts[k] for k in places] + [seconds[k] for k in places])
    args = [own] + arrays
    specs = [VMEM] * len(args)
    alias = {}
    if rhs is not None:
        alias = {len(args): 0}
        args.append(rhs)
        specs.append(pl.BlockSpec(memory_space=pl.ANY))
    return pl.pallas_call(
        functools.partial(stack_kernel, places, near, where),
        out_shape=jax.ShapeDtypeStruct((replicas, depth, width), jnp.bfloat16),
        in_specs=specs,
        out_specs=pl.BlockSpec(memory_space=pl.ANY),
        input_output_aliases=alias,
        scratch_shapes=[
            pltpu.VMEM((count, depth, width), jnp.bfloat16),
            pltpu.SemaphoreType.DMA((count,)),
        ],
        cost_estimate=COST,
        compiler_params=params(),
    )(*args)


def project_kernel(places, near, where, tok_ref, own_ref, base_ref, mom_ref, *refs):
    count = len(places)
    replicas, rows, width = own_ref.shape
    out_hbm, new_base_hbm, new_mom_hbm, rhs_ref, out_ref, sems = refs[-6:]
    stacked_ref = refs[-7]
    me = lax.axis_index("rep")
    copies = [
        pltpu.make_async_copy(base_ref, new_base_hbm, sems.at[replicas]),
        pltpu.make_async_copy(mom_ref, new_mom_hbm, sems.at[replicas + 1]),
    ]
    for copy in copies:
        copy.start()

    def emit(k, rhs):
        out_ref[k] = jnp.dot(tok_ref[...], rhs, preferred_element_type=jnp.float32).astype(
            out_ref.dtype
        )
        copy = pltpu.make_async_copy(
            out_ref.at[k], out_hbm.at[:, columns(me ^ k, width, replicas)], sems.at[k]
        )
        copy.start()
        copies.append(copy)

    for k in range(replicas):
        if k not in places:
            emit(k, stacked_ref[k])
    for i, k in enumerate(places):
        first, second = at_slot(refs, where[i]), at_slot(refs, where[count + i])
        stack(rhs_ref, i, own_ref.at[k], first, second, near)
        emit(k, rhs_ref[i])
    for copy in copies:
        copy.wait()


def project(rhs, tokens, own, new_base, new_mom, firsts, seconds, places, near):
    replicas, rows, width = own.shape
    tall, depth = tokens.shape
    count = len(places)
    arrays, where = gather_slots([firsts[k] for k in places] + [seconds[k] for k in places])
    args = [tokens, own, new_base, new_mom] + arrays
    if rhs is not None:
        args.append(rhs)
    return pl.pallas_call(
        functools.partial(project_kernel, places, near, where),
        out_shape=[
            jax.ShapeDtypeStruct((tall, width * replicas), jnp.bfloat16),
            jax.ShapeDtypeStruct(new_base.shape, jnp.float32),
            jax.ShapeDtypeStruct(new_base.shape, jnp.float32),
        ],
        out_specs=[HBM, HBM, HBM],
        scratch_shapes=[
            pltpu.VMEM((count, depth, width), jnp.bfloat16),
            pltpu.VMEM((replicas, tall, width), jnp.bfloat16),
            pltpu.SemaphoreType.DMA((replicas + 2,)),
        ],
        cost_estimate=COST,
        compiler_params=params(),
    )(*args)


def swap(x, axis, flip):
    return lax.ppermute(x, axis, [(i, i ^ flip) for i in range(lax.axis_size(axis))])


def join_kernel(*refs):
    at = 0
    for ref in refs[:-1]:
        refs[-1][at : at + ref.shape[0], :] = ref[...]
        at += ref.shape[0]


def join(xs):
    return pl.pallas_call(
        join_kernel,
        out_shape=jax.ShapeDtypeStruct((sum(x.shape[0] for x in xs),) + xs[0].shape[1:], xs[0].dtype),
        cost_estimate=COST,
        compiler_params=params(),
    )(*xs)


def pile_kernel(*refs):
    for i, ref in enumerate(refs[:-1]):
        refs[-1][i] = ref[...]


def pile(xs):
    return pl.pallas_call(
        pile_kernel,
        out_shape=jax.ShapeDtypeStruct((len(xs),) + xs[0].shape, xs[0].dtype),
        cost_estimate=COST,
        compiler_params=params(),
    )(*xs)


def share(held, groups):
    slots = {2 * j: (x, None) for j, x in enumerate(held)}
    for group in groups:
        if len(group) == 1:
            slots[2 * group[0] + 1] = (swap(held[group[0]], "rep", 1), None)
        else:
            got = swap(pile([held[j] for j in group]), "rep", 1)
            for i, j in enumerate(group):
                slots[2 * j + 1] = (got, i)
    return [slots[k] for k in range(2 * len(held))]


def after(x, *others):
    return lax.optimization_barrier((x,) + others)[0]


def on_device(base, local, momentum, tokens):
    replicas, groups = lax.axis_size("rep"), lax.axis_size("fsdp")
    chips = replicas // 2
    near = groups // 4
    width = base.shape[1] // replicas

    (send,) = encode(base, local, 1, chips, width)
    recv = swap(send, "rep", 1)
    keep, tokens = encode(base, local, 0, chips, width, tokens)
    sums = chip_sum(keep, recv)
    parts = [swap(sums[j], "rep", 2 * j) for j in range(1, chips)]
    average, fresh = chunk_step(base, momentum, sums[0], parts, replicas)

    far = [swap(fresh, "fsdp", s) for s in range(1, groups)]
    first = join([average] + far[:near])
    second = join(far[near:])
    firsts = [first] + [swap(first, "rep", 2 * j) for j in range(1, chips)]
    seconds = [second] + [swap(second, "rep", 2 * j) for j in range(1, chips)]
    firsts = [first] + [after(x, second) for x in firsts[1:]]
    firsts = share(firsts, [range(chips)])
    new_base, new_momentum, own = outer(base, momentum, firsts, width)
    seconds = share(seconds, [(0, chips - 1)] + [(j,) for j in range(chips - 2, 0, -1)])

    order = [(2 * j, 2 * j + 1) for j in [0] + list(range(chips - 1, 0, -1))]
    rhs = None
    for places in order[:-1]:
        rhs = stacked(rhs, tokens.shape[1], own, firsts, seconds, places, near)
    projected, new_base, new_momentum = project(
        rhs, tokens, own, new_base, new_momentum, firsts, seconds, order[-1], near
    )
    return new_base, new_momentum, projected


def solution(mesh):
    in_specs = (P("fsdp", None), P("rep", "fsdp", None), P("fsdp", None), P(("rep", "fsdp"), None))
    out_specs = (P("fsdp", None), P("fsdp", None), P(("rep", "fsdp"), None))
    return jax.shard_map(
        on_device, mesh=mesh, in_specs=in_specs, out_specs=out_specs, check_vma=False
    )
```

```python
import functools

import jax
import jax.numpy as jnp
from jax import lax
from jax.experimental import pallas as pl
from jax.experimental.pallas import tpu as pltpu
from jax.sharding import PartitionSpec as P

BLOCK = 128
MIB = 1 << 20

outer_lr = 0.7
outer_mu = 0.9

HBM = pl.BlockSpec(memory_space=pltpu.HBM)
VMEM = pl.BlockSpec(memory_space=pltpu.VMEM)
COST = pl.CostEstimate(flops=1 << 34, transcendentals=0, bytes_accessed=1 << 26)


def params(mib=8):
    return pltpu.CompilerParams(vmem_limit_bytes=mib * MIB)


def columns(rep, width, replicas):
    chunk = lax.rem(rep, 2) * (replicas // 2) + lax.div(rep, 2)
    return pl.ds(pl.multiple_of(chunk * width, width), width)


def decoded_block(base, replica):
    delta = base - replica.astype(jnp.float32)
    scale = jnp.max(jnp.abs(delta), axis=1, keepdims=True) + 1e-06
    code = (delta / scale).astype(jnp.bfloat16)
    return (code.astype(jnp.float32) * scale).astype(jnp.bfloat16)


def encode_kernel(flip, base_hbm, local_hbm, *refs):
    *staged, tok_ref, base_ref, local_ref, sems = refs
    out_ref = staged[1] if staged else tok_ref
    chips, rows, width = out_ref.shape
    pieces = sems.shape[1]
    me = lax.axis_index("rep")
    core, chip = lax.rem(me ^ flip, 2), lax.div(me, 2)
    piece = chips * width // pieces
    copies = []
    if staged:
        stage = pltpu.make_async_copy(staged[0], tok_ref, sems.at[2, 0])
    for p in range(pieces):
        here = slice(p * piece, (p + 1) * piece)
        there = pl.ds(pl.multiple_of((core * pieces + p) * piece, piece), piece)
        pair = (
            pltpu.make_async_copy(base_hbm.at[:, there], base_ref.at[:, here], sems.at[0, p]),
            pltpu.make_async_copy(local_hbm.at[0, :, there], local_ref.at[:, here], sems.at[1, p]),
        )
        for copy in pair:
            copy.start()
        copies.append(pair)
    if staged:
        stage.start()
    for p in range(pieces):
        for copy in copies[p]:
            copy.wait()
        for c in range(p * chips // pieces, (p + 1) * chips // pieces):
            for b in range(width // BLOCK):
                cols = slice(c * width + b * BLOCK, c * width + (b + 1) * BLOCK)
                out_ref[chip ^ c, :, b * BLOCK : (b + 1) * BLOCK] = decoded_block(
                    base_ref[:, cols], local_ref[:, cols]
                )
    if staged:
        stage.wait()


def encode(base, local, flip, chips, width, tokens=None):
    rows = base.shape[0]
    base = pltpu.with_memory_space_constraint(base, pltpu.HBM)
    local = pltpu.with_memory_space_constraint(local, pltpu.HBM)
    args, shapes = [base, local], [jax.ShapeDtypeStruct((chips, rows, width), jnp.bfloat16)]
    if tokens is not None:
        args.append(pltpu.with_memory_space_constraint(tokens, pltpu.HBM))
        shapes.append(jax.ShapeDtypeStruct(tokens.shape, tokens.dtype))
    return pl.pallas_call(
        functools.partial(encode_kernel, flip),
        out_shape=shapes,
        in_specs=[HBM] * len(args),
        out_specs=[VMEM] * len(shapes),
        scratch_shapes=[
            pltpu.VMEM((rows, chips * width), jnp.float32),
            pltpu.VMEM((rows, chips * width), jnp.bfloat16),
            pltpu.SemaphoreType.DMA((3, 2)),
        ],
        cost_estimate=COST,
        compiler_params=params(),
    )(*args)


def chip_sum_kernel(keep_ref, recv_ref, *out_refs):
    for j, out_ref in enumerate(out_refs):
        total = keep_ref[j].astype(jnp.float32) + recv_ref[j].astype(jnp.float32)
        out_ref[...] = total.astype(out_ref.dtype)


def chip_sum(keep, recv):
    chips, rows, width = keep.shape
    return pl.pallas_call(
        chip_sum_kernel,
        out_shape=[
            jax.ShapeDtypeStruct((rows, width), jnp.float32 if j == 0 else jnp.bfloat16)
            for j in range(chips)
        ],
        cost_estimate=COST,
        compiler_params=params(),
    )(keep, recv)


def stepped(average, base, momentum):
    moved = outer_mu * momentum + average
    return base - outer_lr * (average + outer_mu * moved), moved


def chunk_step_kernel(replicas, base_ref, mom_ref, own_ref, *refs):
    parts, (avg_ref, fresh_ref) = refs[:-2], refs[-2:]
    cols = columns(lax.axis_index("rep"), own_ref.shape[1], replicas)
    total = own_ref[...]
    for part in parts:
        total = total + part[...].astype(jnp.float32)
    average = (total / replicas).astype(jnp.bfloat16)
    avg_ref[...] = average
    new_base, _ = stepped(average.astype(jnp.float32), base_ref[:, cols], mom_ref[:, cols])
    fresh_ref[...] = new_base.astype(jnp.bfloat16)


def chunk_step(base, momentum, own, parts, replicas):
    return pl.pallas_call(
        functools.partial(chunk_step_kernel, replicas),
        out_shape=[jax.ShapeDtypeStruct(own.shape, jnp.bfloat16)] * 2,
        cost_estimate=COST,
        compiler_params=params(),
    )(base, momentum, own, *parts)


def gather_slots(slots):
    arrays, where = [], []
    for array, place in slots:
        known = [i for i, other in enumerate(arrays) if other is array]
        if not known:
            arrays.append(array)
        where.append((known[0] if known else len(arrays) - 1, place))
    return arrays, where


def at_slot(refs, slot):
    number, place = slot
    return refs[number] if place is None else refs[number].at[place]


def outer_kernel(where, base_ref, mom_ref, *refs):
    holders, (new_base_ref, new_mom_ref, fresh_ref) = refs[:-3], refs[-3:]
    rows, width = fresh_ref.shape[1:]
    me = lax.axis_index("rep")
    for k, slot in enumerate(where):
        cols = columns(me ^ k, width, len(where))
        average = at_slot(holders, slot)[:rows, :].astype(jnp.float32)
        new_base, moved = stepped(average, base_ref[:, cols], mom_ref[:, cols])
        new_base_ref[:, cols] = new_base
        new_mom_ref[:, cols] = moved
        fresh_ref[k] = new_base.astype(jnp.bfloat16)


def outer(base, momentum, firsts, width):
    rows = base.shape[0]
    arrays, where = gather_slots(firsts)
    return pl.pallas_call(
        functools.partial(outer_kernel, where),
        out_shape=[
            jax.ShapeDtypeStruct(base.shape, jnp.float32),
            jax.ShapeDtypeStruct(base.shape, jnp.float32),
            jax.ShapeDtypeStruct((len(firsts), rows, width), jnp.bfloat16),
        ],
        cost_estimate=COST,
        compiler_params=params(),
    )(base, momentum, *arrays)


def stack(rhs_ref, i, own, first, second, near):
    rows = own.shape[0]
    here = lax.axis_index("fsdp")
    pieces = [own[...]]
    pieces += [first[s * rows : (s + 1) * rows, :] for s in range(1, near + 1)]
    pieces += [second[s * rows : (s + 1) * rows, :] for s in range(second.shape[0] // rows)]
    for s, piece in enumerate(pieces):
        rhs_ref[i, pl.ds(pl.multiple_of((here ^ s) * rows, rows), rows), :] = piece


def stack_kernel(places, near, where, own_ref, *refs):
    count = len(places)
    out_ref, rhs_ref, sems = refs[-3:]
    copies = []
    for i, k in enumerate(places):
        first, second = at_slot(refs, where[i]), at_slot(refs, where[count + i])
        stack(rhs_ref, i, own_ref.at[k], first, second, near)
        copies.append(pltpu.make_async_copy(rhs_ref.at[i], out_ref.at[k], sems.at[i]))
        copies[-1].start()
    for copy in copies:
        copy.wait()


def stacked(rhs, depth, own, firsts, seconds, places, near):
    replicas, rows, width = own.shape
    count = len(places)
    arrays, where = gather_slots([firsts[k] for k in places] + [seconds[k] for k in places])
    args = [own] + arrays
    specs = [VMEM] * len(args)
    alias = {}
    if rhs is not None:
        alias = {len(args): 0}
        args.append(rhs)
        specs.append(pl.BlockSpec(memory_space=pl.ANY))
    return pl.pallas_call(
        functools.partial(stack_kernel, places, near, where),
        out_shape=jax.ShapeDtypeStruct((replicas, depth, width), jnp.bfloat16),
        in_specs=specs,
        out_specs=pl.BlockSpec(memory_space=pl.ANY),
        input_output_aliases=alias,
        scratch_shapes=[
            pltpu.VMEM((count, depth, width), jnp.bfloat16),
            pltpu.SemaphoreType.DMA((count,)),
        ],
        cost_estimate=COST,
        compiler_params=params(),
    )(*args)


def project_kernel(places, near, where, tok_ref, own_ref, base_ref, mom_ref, *refs):
    count = len(places)
    replicas, rows, width = own_ref.shape
    out_hbm, new_base_hbm, new_mom_hbm, rhs_ref, out_ref, sems = refs[-6:]
    stacked_ref = refs[-7]
    me = lax.axis_index("rep")
    copies = [
        pltpu.make_async_copy(base_ref, new_base_hbm, sems.at[replicas]),
        pltpu.make_async_copy(mom_ref, new_mom_hbm, sems.at[replicas + 1]),
    ]
    for copy in copies:
        copy.start()

    def emit(k, rhs):
        out_ref[k] = jnp.dot(tok_ref[...], rhs, preferred_element_type=jnp.float32).astype(
            out_ref.dtype
        )
        copy = pltpu.make_async_copy(
            out_ref.at[k], out_hbm.at[:, columns(me ^ k, width, replicas)], sems.at[k]
        )
        copy.start()
        copies.append(copy)

    for k in range(replicas):
        if k not in places:
            emit(k, stacked_ref[k])
    for i, k in enumerate(places):
        first, second = at_slot(refs, where[i]), at_slot(refs, where[count + i])
        stack(rhs_ref, i, own_ref.at[k], first, second, near)
        emit(k, rhs_ref[i])
    for copy in copies:
        copy.wait()


def project(rhs, tokens, own, new_base, new_mom, firsts, seconds, places, near):
    replicas, rows, width = own.shape
    tall, depth = tokens.shape
    count = len(places)
    arrays, where = gather_slots([firsts[k] for k in places] + [seconds[k] for k in places])
    args = [tokens, own, new_base, new_mom] + arrays
    if rhs is not None:
        args.append(rhs)
    return pl.pallas_call(
        functools.partial(project_kernel, places, near, where),
        out_shape=[
            jax.ShapeDtypeStruct((tall, width * replicas), jnp.bfloat16),
            jax.ShapeDtypeStruct(new_base.shape, jnp.float32),
            jax.ShapeDtypeStruct(new_base.shape, jnp.float32),
        ],
        out_specs=[HBM, HBM, HBM],
        scratch_shapes=[
            pltpu.VMEM((count, depth, width), jnp.bfloat16),
            pltpu.VMEM((replicas, tall, width), jnp.bfloat16),
            pltpu.SemaphoreType.DMA((replicas + 2,)),
        ],
        cost_estimate=COST,
        compiler_params=params(),
    )(*args)


def swap(x, axis, flip):
    return lax.ppermute(x, axis, [(i, i ^ flip) for i in range(lax.axis_size(axis))])


def join_kernel(*refs):
    at = 0
    for ref in refs[:-1]:
        refs[-1][at : at + ref.shape[0], :] = ref[...]
        at += ref.shape[0]


def join(xs):
    return pl.pallas_call(
        join_kernel,
        out_shape=jax.ShapeDtypeStruct((sum(x.shape[0] for x in xs),) + xs[0].shape[1:], xs[0].dtype),
        cost_estimate=COST,
        compiler_params=params(),
    )(*xs)


def pile_kernel(*refs):
    for i, ref in enumerate(refs[:-1]):
        refs[-1][i] = ref[...]


def pile(xs):
    return pl.pallas_call(
        pile_kernel,
        out_shape=jax.ShapeDtypeStruct((len(xs),) + xs[0].shape, xs[0].dtype),
        cost_estimate=COST,
        compiler_params=params(),
    )(*xs)


def share(held, groups):
    slots = {2 * j: (x, None) for j, x in enumerate(held)}
    for group in groups:
        if len(group) == 1:
            slots[2 * group[0] + 1] = (swap(held[group[0]], "rep", 1), None)
        else:
            got = swap(pile([held[j] for j in group]), "rep", 1)
            for i, j in enumerate(group):
                slots[2 * j + 1] = (got, i)
    return [slots[k] for k in range(2 * len(held))]


def after(x, *others):
    return lax.optimization_barrier((x,) + others)[0]


def on_device(base, local, momentum, tokens):
    replicas, groups = lax.axis_size("rep"), lax.axis_size("fsdp")
    chips = replicas // 2
    near = groups // 4
    width = base.shape[1] // replicas

    (send,) = encode(base, local, 1, chips, width)
    recv = swap(send, "rep", 1)
    keep, tokens = encode(base, local, 0, chips, width, tokens)
    sums = chip_sum(keep, recv)
    parts = [swap(sums[j], "rep", 2 * j) for j in range(1, chips)]
    average, fresh = chunk_step(base, momentum, sums[0], parts, replicas)

    far = [swap(fresh, "fsdp", s) for s in range(1, groups)]
    first = join([average] + far[:near])
    second = join(far[near:])
    firsts = [first] + [swap(first, "rep", 2 * j) for j in range(1, chips)]
    seconds = [second] + [swap(second, "rep", 2 * j) for j in range(1, chips)]
    firsts = [first] + [after(x, second) for x in firsts[1:]]
    firsts = share(firsts, [range(chips)])
    new_base, new_momentum, own = outer(base, momentum, firsts, width)
    seconds = share(seconds, [(0, chips - 1)] + [(j,) for j in range(chips - 2, 0, -1)])

    order = [(2 * j, 2 * j + 1) for j in [0] + list(range(chips - 1, 0, -1))]
    order = order[1:2] + order[:1] + order[2:]
    rhs = None
    for places in order[:-1]:
        rhs = stacked(rhs, tokens.shape[1], own, firsts, seconds, places, near)
    projected, new_base, new_momentum = project(
        rhs, tokens, own, new_base, new_momentum, firsts, seconds, order[-1], near
    )
    return new_base, new_momentum, projected


def solution(mesh):
    in_specs = (P("fsdp", None), P("rep", "fsdp", None), P("fsdp", None), P(("rep", "fsdp"), None))
    out_specs = (P("fsdp", None), P("fsdp", None), P(("rep", "fsdp"), None))
    return jax.shard_map(
        on_device, mesh=mesh, in_specs=in_specs, out_specs=out_specs, check_vma=False
    )
```
